32 devices in a mesh: ctx: 8 (over y, x, core), dp: 4 (over z).
Axes of the slice: x: 2, y: 2, z: 4, core: 2. Of those that a mesh axis runs over, the one named last changes fastest.
Arguments:
- query: bfloat16 [4, 1536, 4096], P('dp', 'ctx'), may hold values from -6 to 6
- key_value: bfloat16 [4, 1536, 1024], P('dp', 'ctx'), may hold values from -6 to 6
- upstream: bfloat16 [4, 1536, 4096], P('dp', 'ctx'), may hold values from -6 to 6
- log_ratio: float32 [4, 1536], P('dp', 'ctx'), may hold values from -4 to 1
- doc_starts: int32 [4, 16], P('dp'), may hold values from 0 to 1536, as said below
- answer_counts: int32 [4, 16], P('dp'), may hold values from 0 to 768, as said below
Outputs:
- d_query: bfloat16 [4, 1536, 4096], P('dp', 'ctx')
- d_key_value: bfloat16 [4, 1536, 1024], P('dp', 'ctx')
The draws below stay inside these ranges and needn't reach their ends.
Inputs may be any that keep to these rules, and one draw needn't show every extreme that they name: `doc_starts`: used slots come first; each sequence's documents start at the listed positions in rising order, the first at 0, together covering all 1536 positions; unused slots hold 1536; every document has 96 to 768 positions, and every sequence has a document of exactly 768 positions. A document's answer positions are its last answer_counts positions; a used slot holds half of the document's length (rounded down) up to all of it, an unused slot 0; every sequence has a document of 768 positions that are all answer positions.
All inputs are finite; a program needn't handle non-finite values.
Results may differ from the reference program's by a relative error of at most 0.011.
Values may be sent and summed in bfloat16 or wider, within the bound.
A program may use at most 64 MiB of HBM per device.

```python
import jax
import jax.numpy as jnp
from jax import lax

HQ = 32
HK = 4
DH = 128
TOK_DEV = 192
SPAN = 4
LOSS_SCALE = 65536
NSEQ = 4
SEQ = 1536
DOC_MOST = 768
DOC_LEAST = 96
MAXDOC = 16


def doc_layout(key):
    base_key = jax.random.fold_in(key, 11)
    slot_index = jnp.arange(MAXDOC, dtype=jnp.int32)
    fit_count = (SEQ - DOC_LEAST - DOC_MOST) // (DOC_MOST - DOC_LEAST) + 1

    def one_sequence(seq_key):
        length_key, long_key, share_key = jax.random.split(seq_key, 3)
        lengths = jax.random.randint(length_key, (MAXDOC,), DOC_LEAST, DOC_MOST - DOC_LEAST + 1, dtype=jnp.int32)
        longest = jax.random.randint(long_key, (), 0, fit_count, dtype=jnp.int32)
        lengths = jnp.where(slot_index == longest, DOC_MOST, lengths)
        ends_at = jnp.cumsum(lengths)
        starts = ends_at - lengths
        used = starts <= SEQ - DOC_LEAST
        next_used = jnp.concatenate([used[1:], jnp.zeros((1,), jnp.bool_)])
        true_len = jnp.where(next_used, lengths, SEQ - starts)
        shares = jax.random.randint(share_key, (MAXDOC,), 0, 65536, dtype=jnp.int32)
        halves = true_len // 2
        counts = halves + shares * (true_len - halves + 1) // 65536
        counts = jnp.where(slot_index == longest, true_len, counts)
        return (jnp.where(used, starts, SEQ), jnp.where(used, counts, 0))
    return jax.vmap(one_sequence)(jax.random.split(base_key, NSEQ))


def draw_doc_starts(key, part):
    return doc_layout(key)[0].astype(jnp.int32)


def draw_answer_counts(key, part):
    return doc_layout(key)[1].astype(jnp.int32)


def draw_query(key, part):
    result_rows = jnp.clip(jax.random.normal(jax.random.fold_in(key, 31), (NSEQ, SEQ, HQ, DH)), -6.0, 6.0)
    return result_rows.reshape(NSEQ, SEQ, HQ * DH).astype(jnp.bfloat16)


def draw_key_value(key, part):
    stacked = jnp.clip(jax.random.normal(jax.random.fold_in(key, 32), (NSEQ, SEQ, 2, HK, DH)), -6.0, 6.0)
    return stacked.reshape(NSEQ, SEQ, 2 * HK * DH).astype(jnp.bfloat16)


def steps_of(own_key, dims, pieces, smallest, largest):
    def one(dim, parts):
        steps = jax.random.uniform(jax.random.fold_in(jax.random.fold_in(own_key, 6), dim), (parts,), jnp.float32, smallest / len(pieces), largest / len(pieces))
        return jnp.repeat(jnp.exp(steps), dims[dim] // parts).reshape((-1,) + (1,) * (len(dims) - dim - 1))

    level = one(*pieces[0])
    for cut in pieces[1:]:
        level = level * one(*cut)
    return level


def scatter_about(rng, dims, width, limit, cuts=(), held_as=jnp.bfloat16):
    values = width * jax.random.normal(rng, dims, jnp.float32)
    if cuts:
        values = values * steps_of(rng, dims, cuts, -0.22, 0.18)
    return jnp.clip(values, -limit, limit).astype(held_as)


def setup_inputs(seed: int = 0) -> dict:
    keys = jax.random.split(jax.random.key(seed), 7)
    query = draw_query(jax.random.fold_in(keys[6], 71), 0)
    key_value = draw_key_value(jax.random.fold_in(keys[6], 71), 0)
    upstream = scatter_about(keys[2], (NSEQ, SEQ, HQ * DH), 1.0, 6.0, ((0, 4), (1, 8)))
    log_ratio = jnp.clip(-4.0 + 5.0 * jax.random.uniform(keys[3], (NSEQ, SEQ), jnp.float32) ** steps_of(keys[3], (NSEQ, SEQ), ((0, 4), (1, 8)), -0.2, 0.2), -4.0, 1.0)
    doc_starts = draw_doc_starts(jax.random.fold_in(keys[6], 71), 0)
    answer_counts = draw_answer_counts(jax.random.fold_in(keys[6], 71), 0)
    return {"query": query, "key_value": key_value, "upstream": upstream, "log_ratio": log_ratio, "doc_starts": doc_starts, "answer_counts": answer_counts}


def doc_index(starts, positions):
    return jnp.sum((starts[None, :] <= positions[:, None]).astype(jnp.int32), axis=1) - 1


def head_block(query_head, out_grad, key_head, value_head, visible):
    score_scale = DH ** -0.5
    query_wide = query_head.astype(jnp.float32)
    grad_wide = out_grad.astype(jnp.float32)
    key_wide = key_head.astype(jnp.float32)
    value_wide = value_head.astype(jnp.float32)
    scores = jnp.einsum("tgd,kd->gtk", query_wide, key_wide) * score_scale
    scores = jnp.where(visible[None], scores, -1e30)
    row_max = jnp.max(scores, axis=2, keepdims=True)
    row_total = jnp.sum(jnp.exp(scores - row_max), axis=2, keepdims=True)
    prob_full = jnp.exp(scores - (row_max + jnp.log(row_total)))
    prob_low = prob_full.astype(jnp.bfloat16)
    prob_back = prob_low.astype(jnp.float32)
    attended = jnp.einsum("gtk,kd->tgd", prob_back, value_wide)
    row_delta = jnp.sum(grad_wide * attended, axis=2)
    d_probs = jnp.einsum("tgd,kd->gtk", grad_wide, value_wide)
    d_scores = (prob_full * (d_probs - jnp.transpose(row_delta)[:, :, None])).astype(jnp.bfloat16)
    score_back = d_scores.astype(jnp.float32)
    query_grad = jnp.einsum("gtk,kd->tgd", score_back, key_wide) * score_scale
    key_grad = jnp.einsum("gtk,tgd->kd", score_back, query_wide) * score_scale
    value_grad = jnp.einsum("gtk,tgd->kd", prob_back, grad_wide)
    return query_grad, key_grad, value_grad


def sequence_grads(query, key_value, out_grad, doc_of):
    seq_len = query.shape[0]
    kv_width = key_value.shape[1]
    reach = SPAN * TOK_DEV
    window = reach + TOK_DEV
    group_size = HQ // HK
    padded_kv = jnp.concatenate([jnp.zeros((reach, kv_width), key_value.dtype), key_value], axis=0)
    padded_doc = jnp.concatenate([jnp.full((reach,), -1, jnp.int32), doc_of.astype(jnp.int32)], axis=0)

    def step(accum, block):
        first = (block * TOK_DEV).astype(jnp.int32)
        query_rows = lax.dynamic_slice_in_dim(query, first, TOK_DEV, 0)
        grad_rows = lax.dynamic_slice_in_dim(out_grad, first, TOK_DEV, 0)
        doc_rows = lax.dynamic_slice_in_dim(doc_of.astype(jnp.int32), first, TOK_DEV, 0)
        keys_all = lax.dynamic_slice_in_dim(padded_kv, first, window, 0)
        doc_keys = lax.dynamic_slice_in_dim(padded_doc, first, window, 0)
        query_pos = first + jnp.arange(TOK_DEV, dtype=jnp.int32)
        key_pos = first - reach + jnp.arange(window, dtype=jnp.int32)
        visible = (doc_rows[:, None] == doc_keys[None, :]) & (key_pos[None, :] <= query_pos[:, None])
        query_parts = []
        key_parts = []
        value_parts = []
        for head_group in range(HK):
            lo_col = head_group * group_size * DH
            hi_col = lo_col + group_size * DH
            query_head = query_rows[:, lo_col:hi_col].reshape(TOK_DEV, group_size, DH)
            grad_head = grad_rows[:, lo_col:hi_col].reshape(TOK_DEV, group_size, DH)
            key_head = keys_all[:, head_group * DH:(head_group + 1) * DH]
            value_head = keys_all[:, HK * DH + head_group * DH:HK * DH + (head_group + 1) * DH]
            query_grad, key_grad, value_grad = head_block(query_head, grad_head, key_head, value_head, visible)
            query_parts.append(query_grad.reshape(TOK_DEV, group_size * DH))
            key_parts.append(key_grad)
            value_parts.append(value_grad)
        block_grad = jnp.concatenate(key_parts + value_parts, axis=1)
        current = lax.dynamic_slice_in_dim(accum, first, window, 0)
        accum = lax.dynamic_update_slice_in_dim(accum, current + block_grad, first, 0)
        return accum, jnp.concatenate(query_parts, axis=1).astype(jnp.bfloat16)

    start_accum = jnp.zeros((seq_len + reach, kv_width), jnp.float32)
    accum, query_blocks = lax.scan(step, start_accum, jnp.arange(seq_len // TOK_DEV, dtype=jnp.int32))
    return query_blocks.reshape(seq_len, HQ * DH), accum[reach:].astype(jnp.bfloat16)


def reference(query, key_value, upstream, log_ratio, doc_starts, answer_counts):
    seq_len = query.shape[1]
    slot_count = doc_starts.shape[1]
    total_docs = jnp.sum((answer_counts > 0).astype(jnp.float32))
    positions = jnp.arange(seq_len, dtype=jnp.int32)
    slot_index = jnp.arange(slot_count, dtype=jnp.int32)
    query_out = []
    kv_out = []
    for sequence in range(query.shape[0]):
        starts = doc_starts[sequence].astype(jnp.int32)
        counts = answer_counts[sequence].astype(jnp.int32)
        doc_ends = jnp.concatenate([starts[1:], jnp.full((1,), seq_len, jnp.int32)])
        doc_of = doc_index(starts, positions)
        in_doc = doc_of[:, None] == slot_index[None, :]
        end_here = jnp.sum(jnp.where(in_doc, doc_ends[None, :], 0), axis=1)
        count_here = jnp.sum(jnp.where(in_doc, counts[None, :], 0), axis=1)
        answer = positions >= end_here - count_here
        picked = in_doc & answer[:, None]
        doc_sum = jnp.sum(jnp.where(picked, log_ratio[sequence][:, None], 0.0), axis=0)
        floored = jnp.maximum(counts, 1).astype(jnp.float32)
        doc_coef = LOSS_SCALE * 2.0 * jax.nn.sigmoid(doc_sum / floored) / (floored * total_docs)
        weight = jnp.sum(jnp.where(picked, doc_coef[None, :], 0.0), axis=1)
        out_grad = (weight[:, None] * upstream[sequence].astype(jnp.float32)).astype(jnp.bfloat16)
        query_grad, kv_grad = sequence_grads(query[sequence], key_value[sequence], out_grad, doc_of)
        query_out.append(query_grad)
        kv_out.append(kv_grad)
    return jnp.stack(query_out), jnp.stack(kv_out)
```

```python
from functools import partial

import jax
import jax.numpy as jnp
from jax import lax
from jax.experimental import pallas as pl
from jax.experimental.pallas import tpu as pltpu
from jax.sharding import PartitionSpec as P

HQ = 32
HK = 4
DH = 128
SPAN = 4
LOSS_SCALE = 65536
PAIR = 2
MESH_ID = pl.DeviceIdType.MESH
LOG2E = 1.4426950408889634


def as_column(row, shift=0):
    size = row.shape[1]
    r = lax.broadcasted_iota(jnp.int32, (size, size), 0)
    c = lax.broadcasted_iota(jnp.int32, (size, size), 1)
    return jnp.sum(jnp.where(c == r + shift, row, 0.0), axis=1, keepdims=True)


def dot_nt(a, b):
    return lax.dot_general(a, b, (((1,), (1,)), ((), ())), preferred_element_type=jnp.float32)


def kernel(
    n_ctx, n_dp,
    q_ref, kv_ref, up_ref, lr_ref, st_ref, ct_ref,
    dq_ref, dkv_ref,
    kv_all, kt_buf, bias, wcol_ref, acc, gown, gsend, grecv, psend, precv, dsend, drecv,
    kv_ss, kv_rs, g_ss, g_rs, p_ss, p_rs, d_ss, d_rs,
):
    tok = q_ref.shape[0]
    slots = st_ref.shape[1]
    group = HQ // HK
    width = PAIR * tok
    me = lax.axis_index("ctx")
    my_dp = lax.axis_index("dp")
    seq_len = n_ctx * tok
    scale = DH ** (-0.5)

    precv[...] = jnp.zeros_like(precv)

    barrier = pltpu.get_barrier_semaphore()
    for d in range(1, SPAN + 1):
        @pl.when(me + d < n_ctx)
        def _():
            pl.semaphore_signal(barrier, inc=1, device_id={"ctx": me + d}, device_id_type=MESH_ID)

        @pl.when(me >= d)
        def _():
            pl.semaphore_signal(barrier, inc=1, device_id={"ctx": me - d}, device_id_type=MESH_ID)
    for k in range(1, n_dp):
        pl.semaphore_signal(
            barrier, inc=1, device_id={"dp": lax.rem(my_dp + k, n_dp)}, device_id_type=MESH_ID
        )

    for g in range(HK):
        kv_all[g, SPAN * tok:, 0:DH] = kv_ref[:, g * DH:(g + 1) * DH]
        kv_all[g, SPAN * tok:, DH:2 * DH] = kv_ref[:, (HK + g) * DH:(HK + g + 1) * DH]
    for d in range(1, SPAN + 1):
        @pl.when(me < d)
        def _():
            lo = (SPAN - d) * tok
            kv_all[:, lo:lo + tok, :] = jnp.zeros((HK, tok, 2 * DH), jnp.bfloat16)

    starts = as_column(st_ref[...].astype(jnp.float32))
    slot_col = lax.broadcasted_iota(jnp.int32, (slots, 1), 0)
    ends = as_column(st_ref[...].astype(jnp.float32), 1)
    ends = ends + jnp.where(slot_col == slots - 1, jnp.float32(seq_len), 0.0)
    counts_row = ct_ref[...].astype(jnp.float32)
    counts = as_column(counts_row)
    lane = lax.broadcasted_iota(jnp.int32, (1, width), 1)
    pos = (me * tok + jnp.where(lane >= tok, lane - tok, lane)).astype(jnp.float32)
    in_doc = (pos >= starts) & (pos < ends)
    picked = (in_doc & (pos >= ends - counts)).astype(jnp.float32)
    part = jnp.sum(picked[:, :tok] * lr_ref[...], axis=1, keepdims=True)
    psend[...] = jnp.broadcast_to(part, (slots, 128))
    docs = jnp.sum((counts_row > 0).astype(jnp.float32), axis=1, keepdims=True)
    dsend[...] = jnp.broadcast_to(docs, (8, 128))

    pl.semaphore_wait(
        barrier, jnp.minimum(me, SPAN) + jnp.minimum(n_ctx - 1 - me, SPAN) + (n_dp - 1)
    )

    def part_copy(e):
        return pltpu.make_async_remote_copy(
            src_ref=psend, dst_ref=precv.at[SPAN - e],
            send_sem=p_ss.at[SPAN - e], recv_sem=p_rs.at[SPAN - e],
            device_id={"ctx": me + e}, device_id_type=MESH_ID,
        )

    def docs_copy(k):
        return pltpu.make_async_remote_copy(
            src_ref=dsend, dst_ref=drecv.at[k - 1],
            send_sem=d_ss.at[k - 1], recv_sem=d_rs.at[k - 1],
            device_id={"dp": lax.rem(my_dp + k, n_dp)}, device_id_type=MESH_ID,
        )

    def kv_copy(g, d):
        return pltpu.make_async_remote_copy(
            src_ref=kv_all.at[g, pl.ds(SPAN * tok, tok), :],
            dst_ref=kv_all.at[g, pl.ds((SPAN - d) * tok, tok), :],
            send_sem=kv_ss.at[g, SPAN - d], recv_sem=kv_rs.at[g, SPAN - d],
            device_id={"ctx": me + d}, device_id_type=MESH_ID,
        )

    def grad_copy(g, d):
        return pltpu.make_async_remote_copy(
            src_ref=gsend.at[g, SPAN - d], dst_ref=grecv.at[g, SPAN - d],
            send_sem=g_ss.at[g, SPAN - d], recv_sem=g_rs.at[g, SPAN - d],
            device_id={"ctx": me - d}, device_id_type=MESH_ID,
        )

    def can_send(e):
        return me + e < n_ctx if e > 0 else me + e >= 0

    offsets = [e for e in range(-SPAN, SPAN + 1) if e != 0]
    for e in offsets:
        @pl.when(can_send(e))
        def _():
            part_copy(e).start()
    for k in range(1, n_dp):
        docs_copy(k).start()
    for g in range(HK):
        for d in range(1, SPAN + 1):
            @pl.when(me + d < n_ctx)
            def _():
                kv_copy(g, d).start()

    doc_lo = jnp.sum(jnp.where(in_doc, starts, 0.0), axis=0, keepdims=True)
    kpos = (
        (me - SPAN) * tok + lax.broadcasted_iota(jnp.int32, ((SPAN + 1) * tok, 1), 0)
    ).astype(jnp.float32)
    bias[...] = jnp.where((kpos >= doc_lo) & (kpos <= pos), 0.0, -1e30)

    for e in offsets:
        @pl.when(can_send(-e))
        def _():
            part_copy(e).wait_recv()
    for k in range(1, n_dp):
        docs_copy(k).wait_recv()
    doc_sum = psend[...]
    for e in offsets:
        doc_sum = doc_sum + precv[SPAN - e]
    doc_sum = doc_sum[:, 0:1]
    total = dsend[...]
    for k in range(1, n_dp):
        total = total + drecv[k - 1]
    floored = jnp.maximum(counts, 1.0)
    prob = 1.0 / (1.0 + jnp.exp(-(doc_sum / floored)))
    coef = LOSS_SCALE * 2.0 * prob / (floored * total[0:1, 0:1])
    weight = jnp.sum(picked[:, :tok] * coef, axis=0, keepdims=True)
    wcol_ref[...] = jnp.broadcast_to(as_column(weight), (tok, 128))

    def one_group(g, carry):
        for d in range(1, SPAN + 1):
            @pl.when(me >= d)
            def _():
                kv_copy(g, d).wait_recv()
        kt_buf[...] = kv_all[g, :, 0:DH].T
        acc[...] = jnp.zeros_like(acc)

        def one_pair(j, carry):
            first = (g * group + j * PAIR) * DH
            cols = [pl.ds(pl.multiple_of(first + i * DH, DH), DH) for i in range(PAIR)]
            keys = kv_all[g, :, 0:DH]
            vals = kv_all[g, :, DH:2 * DH]
            q2 = jnp.concatenate([q_ref[:, c] for c in cols], axis=0)
            wcol = wcol_ref[...]
            og2 = jnp.concatenate(
                [(wcol * up_ref[:, c].astype(jnp.float32)).astype(jnp.bfloat16) for c in cols],
                axis=0,
            )
            s = dot_nt(keys, q2) * (scale * LOG2E) + bias[...]
            e = jnp.exp2(s - jnp.max(s, axis=0, keepdims=True))
            inv = 1.0 / jnp.sum(e, axis=0, keepdims=True)
            p = e * inv
            dp = dot_nt(vals, og2)
            delta = jnp.sum(p * dp, axis=0, keepdims=True)
            p_low = p.astype(jnp.bfloat16)
            ds = (p * (dp - delta)).astype(jnp.bfloat16)
            dqt = jnp.dot(kt_buf[...], ds, preferred_element_type=jnp.float32) * scale
            dq = dqt.T.astype(jnp.bfloat16)
            for i, c in enumerate(cols):
                dq_ref[:, c] = dq[i * tok:(i + 1) * tok]
            acc[:, 0:DH] += jnp.dot(ds, q2, preferred_element_type=jnp.float32)
            acc[:, DH:2 * DH] += jnp.dot(p_low, og2, preferred_element_type=jnp.float32)
            return carry

        lax.fori_loop(0, group // PAIR, one_pair, 0)
        acc[:, 0:DH] = acc[:, 0:DH] * scale
        for d in range(1, SPAN + 1):
            lo = (SPAN - d) * tok
            @pl.when(me >= d)
            def _():
                gsend[g, SPAN - d] = acc[lo:lo + tok, :].astype(jnp.bfloat16)
                grad_copy(g, d).start()
        gown[g] = acc[SPAN * tok:, :]
        return carry

    lax.fori_loop(0, HK, one_group, 0)

    for g in range(HK):
        for d in range(1, SPAN + 1):
            @pl.when(me + d < n_ctx)
            def _():
                grad_copy(g, d).wait_recv()
                gown[g] += grecv[g, SPAN - d].astype(jnp.float32)
        out = gown[g].astype(jnp.bfloat16)
        dkv_ref[:, g * DH:(g + 1) * DH] = out[:, 0:DH]
        dkv_ref[:, (HK + g) * DH:(HK + g + 1) * DH] = out[:, DH:2 * DH]

    for e in offsets:
        @pl.when(can_send(e))
        def _():
            part_copy(e).wait_send()
    for k in range(1, n_dp):
        docs_copy(k).wait_send()
    for g in range(HK):
        for d in range(1, SPAN + 1):
            @pl.when(me + d < n_ctx)
            def _():
                kv_copy(g, d).wait_send()

            @pl.when(me >= d)
            def _():
                grad_copy(g, d).wait_send()


def local(n_ctx, n_dp, query, key_value, upstream, log_ratio, doc_starts, answer_counts):
    tok = query.shape[1]
    slots = doc_starts.shape[1]
    window = (SPAN + 1) * tok
    f32, bf16 = jnp.float32, jnp.bfloat16
    sem = pltpu.SemaphoreType.DMA
    vmem = pl.BlockSpec(memory_space=pltpu.VMEM)
    flops = 10 * HQ * tok * window * DH
    d_query, d_kv = pl.pallas_call(
        partial(kernel, n_ctx, n_dp),
        out_shape=(
            jax.ShapeDtypeStruct(query.shape[1:], bf16),
            jax.ShapeDtypeStruct(key_value.shape[1:], bf16),
        ),
        in_specs=[vmem] * 6,
        out_specs=(vmem, vmem),
        scratch_shapes=[
            pltpu.VMEM((HK, window, 2 * DH), bf16),
            pltpu.VMEM((DH, window), bf16),
            pltpu.VMEM((window, PAIR * tok), f32),
            pltpu.VMEM((tok, 128), f32),
            pltpu.VMEM((window, 2 * DH), f32),
            pltpu.VMEM((HK, tok, 2 * DH), f32),
            pltpu.VMEM((HK, SPAN, tok, 2 * DH), bf16),
            pltpu.VMEM((HK, SPAN, tok, 2 * DH), bf16),
            pltpu.VMEM((slots, 128), f32),
            pltpu.VMEM((2 * SPAN + 1, slots, 128), f32),
            pltpu.VMEM((8, 128), f32),
            pltpu.VMEM((max(n_dp - 1, 1), 8, 128), f32),
            sem((HK, SPAN)), sem((HK, SPAN)), sem((HK, SPAN)), sem((HK, SPAN)),
            sem((2 * SPAN + 1,)), sem((2 * SPAN + 1,)),
            sem((max(n_dp - 1, 1),)), sem((max(n_dp - 1, 1),)),
        ],
        compiler_params=pltpu.CompilerParams(
            collective_id=0, has_side_effects=True, vmem_limit_bytes=48 * 1024 * 1024
        ),
        cost_estimate=pl.CostEstimate(
            flops=flops, bytes_accessed=8 * 1024 * 1024, transcendentals=HQ * tok * window
        ),
    )(query[0], key_value[0], upstream[0], log_ratio, doc_starts, answer_counts)
    return (d_query[None], d_kv[None])


def solution(mesh):
    n_ctx, n_dp = mesh.shape["ctx"], mesh.shape["dp"]
    return jax.shard_map(
        partial(local, n_ctx, n_dp),
        mesh=mesh,
        in_specs=(
            P("dp", "ctx", None),
            P("dp", "ctx", None),
            P("dp", "ctx", None),
            P("dp", "ctx"),
            P("dp", None),
            P("dp", None),
        ),
        out_specs=(P("dp", "ctx", None), P("dp", "ctx", None)),
        check_vma=False,
    )
```

```python
from functools import partial

import jax
import jax.numpy as jnp
from jax import lax
from jax.experimental import pallas as pl
from jax.experimental.pallas import tpu as pltpu
from jax.sharding import PartitionSpec as P

HQ = 32
HK = 4
DH = 128
SPAN = 4
LOSS_SCALE = 65536
PAIR = 2
MESH_ID = pl.DeviceIdType.MESH
LOG2E = 1.4426950408889634


def as_column(row, shift=0):
    size = row.shape[1]
    r = lax.broadcasted_iota(jnp.int32, (size, size), 0)
    c = lax.broadcasted_iota(jnp.int32, (size, size), 1)
    return jnp.sum(jnp.where(c == r + shift, row, 0.0), axis=1, keepdims=True)


def dot_nt(a, b):
    return lax.dot_general(a, b, (((1,), (1,)), ((), ())), preferred_element_type=jnp.float32)


def kernel(
    n_ctx, n_dp,
    q_hbm, kv_hbm, up_hbm, lr_hbm, st_hbm, ct_hbm,
    dq_ref, dkv_ref,
    q_ref, up_ref, lr_ref, st_ref, ct_ref,
    kv_all, kt_buf, bias, wcol_ref, acc, gown, gsend, xrecv, csend, grecv,
    psend, precv, dsend, drecv,
    in_s, kv_ss, kv_rs, x_ss, x_rs, g_ss, g_rs, p_ss, p_rs, d_ss, d_rs,
):
    tok = q_ref.shape[0]
    slots = st_ref.shape[1]
    group = HQ // HK
    width = PAIR * tok
    me = lax.axis_index("ctx")
    my_dp = lax.axis_index("dp")
    parity = lax.rem(me, 2)
    even = parity == 0
    odd = parity == 1
    partner = me + 1 - 2 * parity
    seq_len = n_ctx * tok
    scale = DH ** (-0.5)

    def small_in():
        pairs = ((st_hbm, st_ref), (ct_hbm, ct_ref), (lr_hbm, lr_ref))
        return [pltpu.make_async_copy(a, b, in_s.at[i]) for i, (a, b) in enumerate(pairs)]

    def kv_in():
        copies = []
        for g in range(HK):
            for i in range(2):
                copies.append(
                    pltpu.make_async_copy(
                        kv_hbm.at[:, pl.ds((i * HK + g) * DH, DH)],
                        kv_all.at[g, pl.ds(SPAN * tok, tok), pl.ds(i * DH, DH)],
                        in_s.at[5 + 2 * g + i],
                    )
                )
        return copies

    def big_in():
        return [
            pltpu.make_async_copy(q_hbm, q_ref, in_s.at[3]),
            pltpu.make_async_copy(up_hbm, up_ref, in_s.at[4]),
        ]

    for c in small_in() + kv_in() + big_in():
        c.start()

    precv[...] = jnp.zeros_like(precv)

    barrier = pltpu.get_barrier_semaphore()
    for d in range(1, SPAN + 1):
        @pl.when(me + d < n_ctx)
        def _():
            pl.semaphore_signal(barrier, inc=1, device_id={"ctx": me + d}, device_id_type=MESH_ID)

        @pl.when(me >= d)
        def _():
            pl.semaphore_signal(barrier, inc=1, device_id={"ctx": me - d}, device_id_type=MESH_ID)
    for k in range(1, n_dp):
        pl.semaphore_signal(
            barrier, inc=1, device_id={"dp": lax.rem(my_dp + k, n_dp)}, device_id_type=MESH_ID
        )

    for d in range(1, SPAN + 1):
        @pl.when(me < d)
        def _():
            lo = (SPAN - d) * tok
            kv_all[:, lo:lo + tok, :] = jnp.zeros((HK, tok, 2 * DH), jnp.bfloat16)

    def remote(src, dst, ss, rs, ctx):
        return pltpu.make_async_remote_copy(
            src_ref=src, dst_ref=dst, send_sem=ss, recv_sem=rs,
            device_id={"ctx": ctx}, device_id_type=MESH_ID,
        )

    def part_copy(e):
        return remote(psend, precv.at[SPAN - e], p_ss.at[SPAN - e], p_rs.at[SPAN - e], me + e)

    def docs_copy(k):
        return pltpu.make_async_remote_copy(
            src_ref=dsend, dst_ref=drecv.at[k - 1],
            send_sem=d_ss.at[k - 1], recv_sem=d_rs.at[k - 1],
            device_id={"dp": lax.rem(my_dp + k, n_dp)}, device_id_type=MESH_ID,
        )

    def kv_slot(g, d):
        return kv_all.at[g, pl.ds((SPAN - d) * tok, tok), :]

    def kv_copy(g, source, dest, index, ctx):
        return remote(
            kv_slot(g, source), kv_slot(g, dest), kv_ss.at[g, index], kv_rs.at[g, SPAN - dest], ctx
        )

    def kv_sends(g):
        return [
            (me + 2 < n_ctx, kv_copy(g, 0, 2, 0, me + 2)),
            (me + 4 < n_ctx, kv_copy(g, 0, 4, 1, me + 4)),
            (even, kv_copy(g, 0, 1, 2, partner)),
        ]

    def kv_forwards(g):
        return [
            (2, even & (me >= 2), kv_copy(g, 2, 3, 3, partner)),
            (2, odd & (me >= 2), kv_copy(g, 2, 1, 3, partner)),
            (4, odd & (me >= 4), kv_copy(g, 4, 3, 4, partner)),
        ]

    def kv_wait(g, d):
        @pl.when(me >= d)
        def _():
            kv_copy(g, 0, d, 0, partner).wait_recv()

    def forward(g):
        for d in (2, 4):
            kv_wait(g, d)
            for source, cond, copy in kv_forwards(g):
                if source == d:
                    pl.when(cond)(copy.start)

    def exchange_copies(g):
        return [
            (even & (me >= 2), remote(gsend.at[g, SPAN - 1], xrecv.at[g, 0], x_ss.at[g, 0], x_rs.at[g, 0], partner)),
            (even & (me >= 2), remote(gsend.at[g, SPAN - 2], xrecv.at[g, 1], x_ss.at[g, 1], x_rs.at[g, 1], partner)),
            (odd & (me >= 4), remote(gsend.at[g, SPAN - 4], xrecv.at[g, 0], x_ss.at[g, 0], x_rs.at[g, 0], partner)),
            (odd, remote(gsend.at[g, SPAN - 1], grecv.at[g, 0], g_ss.at[g, 0], g_rs.at[g, 0], partner)),
            (even & (me >= 4), remote(gsend.at[g, SPAN - 4], grecv.at[g, 2], g_ss.at[g, 0], g_rs.at[g, 2], me - 4)),
        ]

    def final_copies(g):
        return [
            (even & (me >= 4), remote(csend.at[g, 0], grecv.at[g, 2], g_ss.at[g, 1], g_rs.at[g, 2], me - 3)),
            (odd & (me >= 2), remote(csend.at[g, 0], grecv.at[g, 1], g_ss.at[g, 1], g_rs.at[g, 1], me - 2)),
            (odd & (me >= 2), remote(csend.at[g, 1], grecv.at[g, 1], g_ss.at[g, 2], g_rs.at[g, 1], me - 3)),
        ]

    def combine(g):
        def add(i, d):
            both = gsend[g, SPAN - d].astype(jnp.float32) + xrecv[g, i].astype(jnp.float32)
            csend[g, i] = both.astype(jnp.bfloat16)

        @pl.when(even & (me >= 4))
        def _():
            exchange_copies(g)[2][1].wait_recv()
            add(0, 3)
            final_copies(g)[0][1].start()

        @pl.when(odd & (me >= 2))
        def _():
            exchange_copies(g)[0][1].wait_recv()
            add(0, 2)
            final_copies(g)[1][1].start()
            exchange_copies(g)[1][1].wait_recv()
            add(1, 3)
            final_copies(g)[2][1].start()

    for c in small_in():
        c.wait()
    starts = as_column(st_ref[...].astype(jnp.float32))
    slot_col = lax.broadcasted_iota(jnp.int32, (slots, 1), 0)
    ends = as_column(st_ref[...].astype(jnp.float32), 1)
    ends = ends + jnp.where(slot_col == slots - 1, jnp.float32(seq_len), 0.0)
    counts_row = ct_ref[...].astype(jnp.float32)
    counts = as_column(counts_row)
    lane = lax.broadcasted_iota(jnp.int32, (1, width), 1)
    pos = (me * tok + jnp.where(lane >= tok, lane - tok, lane)).astype(jnp.float32)
    in_doc = (pos >= starts) & (pos < ends)
    picked = (in_doc & (pos >= ends - counts)).astype(jnp.float32)
    part = jnp.sum(picked[:, :tok] * lr_ref[...], axis=1, keepdims=True)
    psend[...] = jnp.broadcast_to(part, (slots, 128))
    docs = jnp.sum((counts_row > 0).astype(jnp.float32), axis=1, keepdims=True)
    dsend[...] = jnp.broadcast_to(docs, (8, 128))
    for c in kv_in():
        c.wait()

    pl.semaphore_wait(
        barrier, jnp.minimum(me, SPAN) + jnp.minimum(n_ctx - 1 - me, SPAN) + (n_dp - 1)
    )

    def can_send(e):
        return me + e < n_ctx if e > 0 else me + e >= 0

    offsets = [e for e in range(-SPAN, SPAN + 1) if e != 0]
    for e in offsets:
        @pl.when(can_send(e))
        def _():
            part_copy(e).start()
    for k in range(1, n_dp):
        docs_copy(k).start()
    for g in range(HK):
        for cond, copy in kv_sends(g):
            pl.when(cond)(copy.start)

    doc_lo = jnp.sum(jnp.where(in_doc, starts, 0.0), axis=0, keepdims=True)
    kpos = (
        (me - SPAN) * tok + lax.broadcasted_iota(jnp.int32, ((SPAN + 1) * tok, 1), 0)
    ).astype(jnp.float32)
    bias[...] = jnp.where((kpos >= doc_lo) & (kpos <= pos), 0.0, -1e30)

    for e in offsets:
        @pl.when(can_send(-e))
        def _():
            part_copy(e).wait_recv()
    for k in range(1, n_dp):
        docs_copy(k).wait_recv()
    doc_sum = psend[...]
    for e in offsets:
        doc_sum = doc_sum + precv[SPAN - e]
    doc_sum = doc_sum[:, 0:1]
    total = dsend[...]
    for k in range(1, n_dp):
        total = total + drecv[k - 1]
    floored = jnp.maximum(counts, 1.0)
    prob = 1.0 / (1.0 + jnp.exp(-(doc_sum / floored)))
    coef = LOSS_SCALE * 2.0 * prob / (floored * total[0:1, 0:1])
    weight = jnp.sum(picked[:, :tok] * coef, axis=0, keepdims=True)
    wcol_ref[...] = jnp.broadcast_to(as_column(weight), (tok, 128))
    forward(0)
    for c in big_in():
        c.wait()

    def one_group(g, carry):
        for d in (1, 3):
            kv_wait(g, d)
        kt_buf[...] = kv_all[g, :, 0:DH].T
        acc[...] = jnp.zeros_like(acc)

        def one_pair(j, carry):
            first = (g * group + j * PAIR) * DH
            cols = [pl.ds(pl.multiple_of(first + i * DH, DH), DH) for i in range(PAIR)]
            keys = kv_all[g, :, 0:DH]
            vals = kv_all[g, :, DH:2 * DH]
            q2 = jnp.concatenate([q_ref[:, c] for c in cols], axis=0)
            wcol = wcol_ref[...]
            og2 = jnp.concatenate(
                [(wcol * up_ref[:, c].astype(jnp.float32)).astype(jnp.bfloat16) for c in cols],
                axis=0,
            )
            s = dot_nt(keys, q2) * (scale * LOG2E) + bias[...]
            e = jnp.exp2(s - jnp.max(s, axis=0, keepdims=True))
            inv = 1.0 / jnp.sum(e, axis=0, keepdims=True)
            p = e * inv
            dp = dot_nt(vals, og2)
            delta = jnp.sum(p * dp, axis=0, keepdims=True)
            p_low = p.astype(jnp.bfloat16)
            ds = (p * (dp - delta)).astype(jnp.bfloat16)
            dqt = jnp.dot(kt_buf[...], ds, preferred_element_type=jnp.float32) * scale
            dq = dqt.T.astype(jnp.bfloat16)
            for i, c in enumerate(cols):
                dq_ref[:, c] = dq[i * tok:(i + 1) * tok]
            acc[:, 0:DH] += jnp.dot(ds, q2, preferred_element_type=jnp.float32)
            acc[:, DH:2 * DH] += jnp.dot(p_low, og2, preferred_element_type=jnp.float32)

            @pl.when((j == 0) & (g > 0))
            def _():
                combine(g - 1)

            @pl.when((j == group // PAIR - 2) & (g < HK - 1))
            def _():
                forward(g + 1)

            return carry

        lax.fori_loop(0, group // PAIR, one_pair, 0)
        for d in range(1, SPAN + 1):
            lo = (SPAN - d) * tok
            gsend[g, SPAN - d, :, 0:DH] = (acc[lo:lo + tok, 0:DH] * scale).astype(jnp.bfloat16)
            gsend[g, SPAN - d, :, DH:2 * DH] = acc[lo:lo + tok, DH:2 * DH].astype(jnp.bfloat16)
        for cond, copy in exchange_copies(g):
            pl.when(cond)(copy.start)
        gown[g, :, 0:DH] = acc[SPAN * tok:, 0:DH] * scale
        gown[g, :, DH:2 * DH] = acc[SPAN * tok:, DH:2 * DH]
        return carry

    lax.fori_loop(0, HK, one_group, 0)
    combine(HK - 1)

    for g in range(HK):
        arrivals = ((0, even), (1, me - parity + 2 < n_ctx), (2, me - parity + 4 < n_ctx))
        for slot, cond in arrivals:
            @pl.when(cond)
            def _():
                remote(
                    csend.at[g, 0], grecv.at[g, slot], g_ss.at[g, 0], g_rs.at[g, slot], partner
                ).wait_recv()
                gown[g] += grecv[g, slot].astype(jnp.float32)
        out = gown[g].astype(jnp.bfloat16)
        dkv_ref[:, g * DH:(g + 1) * DH] = out[:, 0:DH]
        dkv_ref[:, (HK + g) * DH:(HK + g + 1) * DH] = out[:, DH:2 * DH]

    for e in offsets:
        @pl.when(can_send(e))
        def _():
            part_copy(e).wait_send()
    for k in range(1, n_dp):
        docs_copy(k).wait_send()
    for g in range(HK):
        sent = kv_sends(g) + [f[1:] for f in kv_forwards(g)] + exchange_copies(g) + final_copies(g)
        for cond, copy in sent:
            pl.when(cond)(copy.wait_send)


def local(n_ctx, n_dp, query, key_value, upstream, log_ratio, doc_starts, answer_counts):
    tok = query.shape[1]
    slots = doc_starts.shape[1]
    window = (SPAN + 1) * tok
    f32, bf16 = jnp.float32, jnp.bfloat16
    sem = pltpu.SemaphoreType.DMA
    vmem = pl.BlockSpec(memory_space=pltpu.VMEM)
    flops = 10 * HQ * tok * window * DH
    d_query, d_kv = pl.pallas_call(
        partial(kernel, n_ctx, n_dp),
        out_shape=(
            jax.ShapeDtypeStruct(query.shape[1:], bf16),
            jax.ShapeDtypeStruct(key_value.shape[1:], bf16),
        ),
        in_specs=[pl.BlockSpec(memory_space=pltpu.HBM)] * 6,
        out_specs=(vmem, vmem),
        scratch_shapes=[
            pltpu.VMEM(query.shape[1:], bf16),
            pltpu.VMEM(upstream.shape[1:], bf16),
            pltpu.VMEM(log_ratio.shape, f32),
            pltpu.VMEM(doc_starts.shape, jnp.int32),
            pltpu.VMEM(answer_counts.shape, jnp.int32),
            pltpu.VMEM((HK, window, 2 * DH), bf16),
            pltpu.VMEM((DH, window), bf16),
            pltpu.VMEM((window, PAIR * tok), f32),
            pltpu.VMEM((tok, 128), f32),
            pltpu.VMEM((window, 2 * DH), f32),
            pltpu.VMEM((HK, tok, 2 * DH), f32),
            pltpu.VMEM((HK, SPAN, tok, 2 * DH), bf16),
            pltpu.VMEM((HK, 2, tok, 2 * DH), bf16),
            pltpu.VMEM((HK, 2, tok, 2 * DH), bf16),
            pltpu.VMEM((HK, 3, tok, 2 * DH), bf16),
            pltpu.VMEM((slots, 128), f32),
            pltpu.VMEM((2 * SPAN + 1, slots, 128), f32),
            pltpu.VMEM((8, 128), f32),
            pltpu.VMEM((max(n_dp - 1, 1), 8, 128), f32),
            sem((5 + 2 * HK,)), sem((HK, 5)), sem((HK, SPAN)),
            sem((HK, 2)), sem((HK, 2)), sem((HK, 3)), sem((HK, 3)),
            sem((2 * SPAN + 1,)), sem((2 * SPAN + 1,)),
            sem((max(n_dp - 1, 1),)), sem((max(n_dp - 1, 1),)),
        ],
        compiler_params=pltpu.CompilerParams(
            collective_id=0, has_side_effects=True, vmem_limit_bytes=48 * 1024 * 1024
        ),
        cost_estimate=pl.CostEstimate(
            flops=flops, bytes_accessed=8 * 1024 * 1024, transcendentals=HQ * tok * window
        ),
    )(query[0], key_value[0], upstream[0], log_ratio, doc_starts, answer_counts)
    return (d_query[None], d_kv[None])


def solution(mesh):
    n_ctx, n_dp = mesh.shape["ctx"], mesh.shape["dp"]
    return jax.shard_map(
        partial(local, n_ctx, n_dp),
        mesh=mesh,
        in_specs=(
            P("dp", "ctx", None),
            P("dp", "ctx", None),
            P("dp", "ctx", None),
            P("dp", "ctx"),
            P("dp", None),
            P("dp", None),
        ),
        out_specs=(P("dp", "ctx", None), P("dp", "ctx", None)),
        check_vma=False,
    )
```

```python
from functools import partial

import jax
import jax.numpy as jnp
from jax import lax
from jax.experimental import pallas as pl
from jax.experimental.pallas import tpu as pltpu
from jax.sharding import PartitionSpec as P

HQ = 32
HK = 4
DH = 128
SPAN = 4
LOSS_SCALE = 65536
PAIR = 4
MESH_ID = pl.DeviceIdType.MESH
LOG2E = 1.4426950408889634


def as_column(row, shift=0):
    size = row.shape[1]
    r = lax.broadcasted_iota(jnp.int32, (size, size), 0)
    c = lax.broadcasted_iota(jnp.int32, (size, size), 1)
    return jnp.sum(jnp.where(c == r + shift, row, 0.0), axis=1, keepdims=True)


def dot_nt(a, b):
    return lax.dot_general(a, b, (((1,), (1,)), ((), ())), preferred_element_type=jnp.float32)


def kernel(
    n_ctx, n_dp,
    q_hbm, kv_hbm, up_hbm, lr_hbm, st_hbm, ct_hbm,
    dq_hbm, dkv_hbm,
    dq_ref, dkv_ref, q_ref, up_ref, lr_ref, st_ref, ct_ref,
    kv_all, kt_buf, bias, wcol_ref, acc, gown, gsend, xrecv, csend, grecv,
    psend, precv, dsend, drecv,
    in_s, out_s, kv_ss, kv_rs, x_ss, x_rs, g_ss, g_rs, p_ss, p_rs, d_ss, d_rs,
):
    tok = q_ref.shape[0]
    slots = st_ref.shape[1]
    group = HQ // HK
    width = PAIR * tok
    me = lax.axis_index("ctx")
    my_dp = lax.axis_index("dp")
    parity = lax.rem(me, 2)
    even = parity == 0
    odd = parity == 1
    partner = me + 1 - 2 * parity
    seq_len = n_ctx * tok
    scale = DH ** (-0.5)

    def small_in():
        pairs = ((st_hbm, st_ref), (ct_hbm, ct_ref), (lr_hbm, lr_ref))
        return [pltpu.make_async_copy(a, b, in_s.at[i]) for i, (a, b) in enumerate(pairs)]

    def kv_in():
        copies = []
        for g in range(HK):
            for i in range(2):
                copies.append(
                    pltpu.make_async_copy(
                        kv_hbm.at[:, pl.ds((i * HK + g) * DH, DH)],
                        kv_all.at[g, pl.ds(SPAN * tok, tok), pl.ds(i * DH, DH)],
                        in_s.at[5 + 2 * g + i],
                    )
                )
        return copies

    def big_in():
        return [
            pltpu.make_async_copy(q_hbm, q_ref, in_s.at[3]),
            pltpu.make_async_copy(up_hbm, up_ref, in_s.at[4]),
        ]

    for c in small_in() + kv_in() + big_in():
        c.start()

    precv[...] = jnp.zeros_like(precv)

    barrier = pltpu.get_barrier_semaphore()
    for d in range(1, SPAN + 1):
        @pl.when(me + d < n_ctx)
        def _():
            pl.semaphore_signal(barrier, inc=1, device_id={"ctx": me + d}, device_id_type=MESH_ID)

        @pl.when(me >= d)
        def _():
            pl.semaphore_signal(barrier, inc=1, device_id={"ctx": me - d}, device_id_type=MESH_ID)
    for k in range(1, n_dp):
        pl.semaphore_signal(
            barrier, inc=1, device_id={"dp": lax.rem(my_dp + k, n_dp)}, device_id_type=MESH_ID
        )

    for d in range(1, SPAN + 1):
        @pl.when(me < d)
        def _():
            lo = (SPAN - d) * tok
            kv_all[:, lo:lo + tok, :] = jnp.zeros((HK, tok, 2 * DH), jnp.bfloat16)

    def remote(src, dst, ss, rs, ctx):
        return pltpu.make_async_remote_copy(
            src_ref=src, dst_ref=dst, send_sem=ss, recv_sem=rs,
            device_id={"ctx": ctx}, device_id_type=MESH_ID,
        )

    def part_copy(e):
        return remote(psend, precv.at[SPAN - e], p_ss.at[SPAN - e], p_rs.at[SPAN - e], me + e)

    def docs_copy(k):
        return pltpu.make_async_remote_copy(
            src_ref=dsend, dst_ref=drecv.at[k - 1],
            send_sem=d_ss.at[k - 1], recv_sem=d_rs.at[k - 1],
            device_id={"dp": lax.rem(my_dp + k, n_dp)}, device_id_type=MESH_ID,
        )

    def kv_slot(g, d):
        return kv_all.at[g, pl.ds((SPAN - d) * tok, tok), :]

    def kv_copy(g, source, dest, index, ctx):
        return remote(
            kv_slot(g, source), kv_slot(g, dest), kv_ss.at[g, index], kv_rs.at[g, SPAN - dest], ctx
        )

    def kv_sends(g):
        return [
            (me + 2 < n_ctx, kv_copy(g, 0, 2, 0, me + 2)),
            (me + 4 < n_ctx, kv_copy(g, 0, 4, 1, me + 4)),
            (even, kv_copy(g, 0, 1, 2, partner)),
        ]

    def kv_forwards(g):
        return [
            (2, even & (me >= 2), kv_copy(g, 2, 3, 3, partner)),
            (2, odd & (me >= 2), kv_copy(g, 2, 1, 3, partner)),
            (4, odd & (me >= 4), kv_copy(g, 4, 3, 4, partner)),
        ]

    def kv_wait(g, d):
        @pl.when(me >= d)
        def _():
            kv_copy(g, 0, d, 0, partner).wait_recv()

    def forward(g):
        for d in (2, 4):
            kv_wait(g, d)
            for source, cond, copy in kv_forwards(g):
                if source == d:
                    pl.when(cond)(copy.start)

    def exchange_copies(g):
        return [
            (even & (me >= 2), remote(gsend.at[g, SPAN - 1], xrecv.at[g, 0], x_ss.at[g, 0], x_rs.at[g, 0], partner)),
            (even & (me >= 2), remote(gsend.at[g, SPAN - 2], xrecv.at[g, 1], x_ss.at[g, 1], x_rs.at[g, 1], partner)),
            (odd & (me >= 4), remote(gsend.at[g, SPAN - 4], xrecv.at[g, 0], x_ss.at[g, 0], x_rs.at[g, 0], partner)),
            (odd, remote(gsend.at[g, SPAN - 1], grecv.at[g, 0], g_ss.at[g, 0], g_rs.at[g, 0], partner)),
            (even & (me >= 4), remote(gsend.at[g, SPAN - 4], grecv.at[g, 2], g_ss.at[g, 0], g_rs.at[g, 2], me - 4)),
        ]

    def final_copies(g):
        return [
            (even & (me >= 4), remote(csend.at[g, 0], grecv.at[g, 2], g_ss.at[g, 1], g_rs.at[g, 2], me - 3)),
            (odd & (me >= 2), remote(csend.at[g, 0], grecv.at[g, 1], g_ss.at[g, 1], g_rs.at[g, 1], me - 2)),
            (odd & (me >= 2), remote(csend.at[g, 1], grecv.at[g, 1], g_ss.at[g, 2], g_rs.at[g, 1], me - 3)),
        ]

    def combine(g):
        def add(i, d):
            both = gsend[g, SPAN - d].astype(jnp.float32) + xrecv[g, i].astype(jnp.float32)
            csend[g, i] = both.astype(jnp.bfloat16)

        @pl.when(even & (me >= 4))
        def _():
            exchange_copies(g)[2][1].wait_recv()
            add(0, 3)
            final_copies(g)[0][1].start()

        @pl.when(odd & (me >= 2))
        def _():
            exchange_copies(g)[0][1].wait_recv()
            add(0, 2)
            final_copies(g)[1][1].start()
            exchange_copies(g)[1][1].wait_recv()
            add(1, 3)
            final_copies(g)[2][1].start()

    def dq_out(g):
        cols = pl.ds(pl.multiple_of(g * (group * DH), DH), group * DH)
        return pltpu.make_async_copy(dq_ref.at[:, cols], dq_hbm.at[:, cols], out_s.at[g])

    for c in small_in():
        c.wait()
    starts = as_column(st_ref[...].astype(jnp.float32))
    slot_col = lax.broadcasted_iota(jnp.int32, (slots, 1), 0)
    ends = as_column(st_ref[...].astype(jnp.float32), 1)
    ends = ends + jnp.where(slot_col == slots - 1, jnp.float32(seq_len), 0.0)
    counts_row = ct_ref[...].astype(jnp.float32)
    counts = as_column(counts_row)
    lane = lax.rem(lax.broadcasted_iota(jnp.int32, (1, width), 1), tok)
    pos = (me * tok + lane).astype(jnp.float32)
    in_doc = (pos >= starts) & (pos < ends)
    picked = (in_doc & (pos >= ends - counts)).astype(jnp.float32)
    part = jnp.sum(picked[:, :tok] * lr_ref[...], axis=1, keepdims=True)
    psend[...] = jnp.broadcast_to(part, (slots, 128))
    docs = jnp.sum((counts_row > 0).astype(jnp.float32), axis=1, keepdims=True)
    dsend[...] = jnp.broadcast_to(docs, (8, 128))
    for c in kv_in():
        c.wait()

    pl.semaphore_wait(
        barrier, jnp.minimum(me, SPAN) + jnp.minimum(n_ctx - 1 - me, SPAN) + (n_dp - 1)
    )

    def can_send(e):
        return me + e < n_ctx if e > 0 else me + e >= 0

    offsets = [e for e in range(-SPAN, SPAN + 1) if e != 0]
    for e in offsets:
        @pl.when(can_send(e))
        def _():
            part_copy(e).start()
    for k in range(1, n_dp):
        docs_copy(k).start()
    for g in range(HK):
        for cond, copy in kv_sends(g):
            pl.when(cond)(copy.start)

    doc_lo = jnp.sum(jnp.where(in_doc, starts, 0.0), axis=0, keepdims=True)
    kpos = (
        (me - SPAN) * tok + lax.broadcasted_iota(jnp.int32, ((SPAN + 1) * tok, 1), 0)
    ).astype(jnp.float32)
    bias[...] = jnp.where((kpos >= doc_lo) & (kpos <= pos), 0.0, -1e30)

    for e in offsets:
        @pl.when(can_send(-e))
        def _():
            part_copy(e).wait_recv()
    for k in range(1, n_dp):
        docs_copy(k).wait_recv()
    doc_sum = psend[...]
    for e in offsets:
        doc_sum = doc_sum + precv[SPAN - e]
    doc_sum = doc_sum[:, 0:1]
    total = dsend[...]
    for k in range(1, n_dp):
        total = total + drecv[k - 1]
    floored = jnp.maximum(counts, 1.0)
    prob = 1.0 / (1.0 + jnp.exp(-(doc_sum / floored)))
    coef = LOSS_SCALE * 2.0 * prob / (floored * total[0:1, 0:1])
    weight = jnp.sum(picked[:, :tok] * coef, axis=0, keepdims=True)
    wcol_ref[...] = jnp.broadcast_to(as_column(weight), (tok, 128))
    forward(0)
    for c in big_in():
        c.wait()

    def one_group(g, carry):
        for d in (1, 3):
            kv_wait(g, d)
        kt_buf[...] = kv_all[g, :, 0:DH].T
        acc[...] = jnp.zeros_like(acc)

        def one_pair(j, carry):
            first = (g * group + j * PAIR) * DH
            cols = [pl.ds(pl.multiple_of(first + i * DH, DH), DH) for i in range(PAIR)]
            keys = kv_all[g, :, 0:DH]
            vals = kv_all[g, :, DH:2 * DH]
            q2 = jnp.concatenate([q_ref[:, c] for c in cols], axis=0)
            wcol = wcol_ref[...]
            og2 = jnp.concatenate(
                [(wcol * up_ref[:, c].astype(jnp.float32)).astype(jnp.bfloat16) for c in cols],
                axis=0,
            )
            s = dot_nt(keys, q2) * (scale * LOG2E) + bias[...]
            e = jnp.exp2(s - jnp.max(s, axis=0, keepdims=True))
            inv = 1.0 / jnp.sum(e, axis=0, keepdims=True)
            p = e * inv
            dp = dot_nt(vals, og2)
            delta = jnp.sum(p * dp, axis=0, keepdims=True)
            p_low = p.astype(jnp.bfloat16)
            ds = (p * (dp - delta)).astype(jnp.bfloat16)
            dqt = jnp.dot(kt_buf[...], ds, preferred_element_type=jnp.float32) * scale
            dq = dqt.T.astype(jnp.bfloat16)
            for i, c in enumerate(cols):
                dq_ref[:, c] = dq[i * tok:(i + 1) * tok]
            acc[:, 0:DH] += jnp.dot(ds, q2, preferred_element_type=jnp.float32)
            acc[:, DH:2 * DH] += jnp.dot(p_low, og2, preferred_element_type=jnp.float32)

            @pl.when((j == 0) & (g > 0))
            def _():
                combine(g - 1)

            @pl.when((j == group // PAIR - 2) & (g < HK - 1))
            def _():
                forward(g + 1)

            return carry

        lax.fori_loop(0, group // PAIR, one_pair, 0)
        dq_out(g).start()
        for d in range(1, SPAN + 1):
            lo = (SPAN - d) * tok
            gsend[g, SPAN - d, :, 0:DH] = (acc[lo:lo + tok, 0:DH] * scale).astype(jnp.bfloat16)
            gsend[g, SPAN - d, :, DH:2 * DH] = acc[lo:lo + tok, DH:2 * DH].astype(jnp.bfloat16)
        for cond, copy in exchange_copies(g):
            pl.when(cond)(copy.start)
        gown[g, :, 0:DH] = acc[SPAN * tok:, 0:DH] * scale
        gown[g, :, DH:2 * DH] = acc[SPAN * tok:, DH:2 * DH]
        return carry

    lax.fori_loop(0, HK, one_group, 0)
    combine(HK - 1)

    for g in range(HK):
        arrivals = ((0, even), (1, me - parity + 2 < n_ctx), (2, me - parity + 4 < n_ctx))
        for slot, cond in arrivals:
            @pl.when(cond)
            def _():
                remote(
                    csend.at[g, 0], grecv.at[g, slot], g_ss.at[g, 0], g_rs.at[g, slot], partner
                ).wait_recv()
                gown[g] += grecv[g, slot].astype(jnp.float32)
        out = gown[g].astype(jnp.bfloat16)
        dkv_ref[:, g * DH:(g + 1) * DH] = out[:, 0:DH]
        dkv_ref[:, (HK + g) * DH:(HK + g + 1) * DH] = out[:, DH:2 * DH]

    dkv_out = pltpu.make_async_copy(dkv_ref, dkv_hbm, out_s.at[HK])
    dkv_out.start()
    for e in offsets:
        @pl.when(can_send(e))
        def _():
            part_copy(e).wait_send()
    for k in range(1, n_dp):
        docs_copy(k).wait_send()
    for g in range(HK):
        sent = kv_sends(g) + [f[1:] for f in kv_forwards(g)] + exchange_copies(g) + final_copies(g)
        for cond, copy in sent:
            pl.when(cond)(copy.wait_send)
        dq_out(g).wait()
    dkv_out.wait()


def local(n_ctx, n_dp, query, key_value, upstream, log_ratio, doc_starts, answer_counts):
    tok = query.shape[1]
    slots = doc_starts.shape[1]
    window = (SPAN + 1) * tok
    f32, bf16 = jnp.float32, jnp.bfloat16
    sem = pltpu.SemaphoreType.DMA
    hbm = pl.BlockSpec(memory_space=pltpu.HBM)
    flops = 10 * HQ * tok * window * DH
    d_query, d_kv = pl.pallas_call(
        partial(kernel, n_ctx, n_dp),
        out_shape=(
            jax.ShapeDtypeStruct(query.shape[1:], bf16),
            jax.ShapeDtypeStruct(key_value.shape[1:], bf16),
        ),
        in_specs=[hbm] * 6,
        out_specs=(hbm, hbm),
        scratch_shapes=[
            pltpu.VMEM(query.shape[1:], bf16),
            pltpu.VMEM(key_value.shape[1:], bf16),
            pltpu.VMEM(query.shape[1:], bf16),
            pltpu.VMEM(upstream.shape[1:], bf16),
            pltpu.VMEM(log_ratio.shape, f32),
            pltpu.VMEM(doc_starts.shape, jnp.int32),
            pltpu.VMEM(answer_counts.shape, jnp.int32),
            pltpu.VMEM((HK, window, 2 * DH), bf16),
            pltpu.VMEM((DH, window), bf16),
            pltpu.VMEM((window, PAIR * tok), f32),
            pltpu.VMEM((tok, 128), f32),
            pltpu.VMEM((window, 2 * DH), f32),
            pltpu.VMEM((HK, tok, 2 * DH), f32),
            pltpu.VMEM((HK, SPAN, tok, 2 * DH), bf16),
            pltpu.VMEM((HK, 2, tok, 2 * DH), bf16),
            pltpu.VMEM((HK, 2, tok, 2 * DH), bf16),
            pltpu.VMEM((HK, 3, tok, 2 * DH), bf16),
            pltpu.VMEM((slots, 128), f32),
            pltpu.VMEM((2 * SPAN + 1, slots, 128), f32),
            pltpu.VMEM((8, 128), f32),
            pltpu.VMEM((max(n_dp - 1, 1), 8, 128), f32),
            sem((5 + 2 * HK,)), sem((HK + 1,)), sem((HK, 5)), sem((HK, SPAN)),
            sem((HK, 2)), sem((HK, 2)), sem((HK, 3)), sem((HK, 3)),
            sem((2 * SPAN + 1,)), sem((2 * SPAN + 1,)),
            sem((max(n_dp - 1, 1),)), sem((max(n_dp - 1, 1),)),
        ],
        compiler_params=pltpu.CompilerParams(
            collective_id=0, has_side_effects=True, vmem_limit_bytes=64 * 1024 * 1024
        ),
        cost_estimate=pl.CostEstimate(
            flops=flops, bytes_accessed=8 * 1024 * 1024, transcendentals=HQ * tok * window
        ),
    )(query[0], key_value[0], upstream[0], log_ratio, doc_starts, answer_counts)
    return (d_query[None], d_kv[None])


def solution(mesh):
    n_ctx, n_dp = mesh.shape["ctx"], mesh.shape["dp"]
    return jax.shard_map(
        partial(local, n_ctx, n_dp),
        mesh=mesh,
        in_specs=(
            P("dp", "ctx", None),
            P("dp", "ctx", None),
            P("dp", "ctx", None),
            P("dp", "ctx"),
            P("dp", None),
            P("dp", None),
        ),
        out_specs=(P("dp", "ctx", None), P("dp", "ctx", None)),
        check_vma=False,
    )
```

```python
from functools import partial

import jax
import jax.numpy as jnp
from jax import lax
from jax.experimental import pallas as pl
from jax.experimental.pallas import tpu as pltpu
from jax.sharding import PartitionSpec as P

HQ = 32
HK = 4
DH = 128
SPAN = 4
LOSS_SCALE = 65536
PAIR = 4
MESH_ID = pl.DeviceIdType.MESH
LOG2E = 1.4426950408889634


def as_column(row, shift=0):
    size = row.shape[1]
    r = lax.broadcasted_iota(jnp.int32, (size, size), 0)
    c = lax.broadcasted_iota(jnp.int32, (size, size), 1)
    return jnp.sum(jnp.where(c == r + shift, row, 0.0), axis=1, keepdims=True)


def dot_nt(a, b):
    return lax.dot_general(a, b, (((1,), (1,)), ((), ())), preferred_element_type=jnp.float32)


def kernel(
    n_ctx, n_dp,
    q_hbm, kv_hbm, up_hbm, lr_hbm, st_hbm, ct_hbm,
    dq_hbm, dkv_hbm,
    dq_ref, dkv_ref, q_ref, up_ref, lr_ref, st_ref, ct_ref,
    kv_all, kt_buf, bias, wcol_ref, acc, gown, gsend, xrecv, csend, grecv,
    psend, precv, dsend, drecv,
    in_s, out_s, kv_ss, kv_rs, x_ss, x_rs, g_ss, g_rs, p_ss, p_rs, d_ss, d_rs,
):
    tok = q_ref.shape[0]
    slots = st_ref.shape[1]
    group = HQ // HK
    width = PAIR * tok
    me = lax.axis_index("ctx")
    my_dp = lax.axis_index("dp")
    parity = lax.rem(me, 2)
    even = parity == 0
    odd = parity == 1
    partner = me + 1 - 2 * parity
    seq_len = n_ctx * tok
    scale = DH ** (-0.5)

    def small_in():
        pairs = ((st_hbm, st_ref), (ct_hbm, ct_ref), (lr_hbm, lr_ref))
        return [pltpu.make_async_copy(a, b, in_s.at[i]) for i, (a, b) in enumerate(pairs)]

    def kv_in():
        copies = []
        for g in range(HK):
            for i in range(2):
                copies.append(
                    pltpu.make_async_copy(
                        kv_hbm.at[:, pl.ds((i * HK + g) * DH, DH)],
                        kv_all.at[g, pl.ds(SPAN * tok, tok), pl.ds(i * DH, DH)],
                        in_s.at[5 + 2 * g + i],
                    )
                )
        return copies

    def big_in():
        return [
            pltpu.make_async_copy(q_hbm, q_ref, in_s.at[3]),
            pltpu.make_async_copy(up_hbm, up_ref, in_s.at[4]),
        ]

    for c in small_in() + kv_in() + big_in():
        c.start()

    precv[...] = jnp.zeros_like(precv)

    barrier = pltpu.get_barrier_semaphore()
    for d in range(1, SPAN + 1):
        @pl.when(me + d < n_ctx)
        def _():
            pl.semaphore_signal(barrier, inc=1, device_id={"ctx": me + d}, device_id_type=MESH_ID)

        @pl.when(me >= d)
        def _():
            pl.semaphore_signal(barrier, inc=1, device_id={"ctx": me - d}, device_id_type=MESH_ID)
    for k in range(1, n_dp):
        pl.semaphore_signal(
            barrier, inc=1, device_id={"dp": lax.rem(my_dp + k, n_dp)}, device_id_type=MESH_ID
        )

    for d in range(1, SPAN + 1):
        @pl.when(me < d)
        def _():
            lo = (SPAN - d) * tok
            kv_all[:, lo:lo + tok, :] = jnp.zeros((HK, tok, 2 * DH), jnp.bfloat16)

    def remote(src, dst, ss, rs, ctx):
        return pltpu.make_async_remote_copy(
            src_ref=src, dst_ref=dst, send_sem=ss, recv_sem=rs,
            device_id={"ctx": ctx}, device_id_type=MESH_ID,
        )

    def part_copy(e):
        return remote(psend, precv.at[SPAN - e], p_ss.at[SPAN - e], p_rs.at[SPAN - e], me + e)

    def docs_copy(k):
        return pltpu.make_async_remote_copy(
            src_ref=dsend, dst_ref=drecv.at[k - 1],
            send_sem=d_ss.at[k - 1], recv_sem=d_rs.at[k - 1],
            device_id={"dp": lax.rem(my_dp + k, n_dp)}, device_id_type=MESH_ID,
        )

    def kv_slot(g, d):
        return kv_all.at[g, pl.ds((SPAN - d) * tok, tok), :]

    def kv_copy(g, source, dest, index, ctx):
        return remote(
            kv_slot(g, source), kv_slot(g, dest), kv_ss.at[g, index], kv_rs.at[g, SPAN - dest], ctx
        )

    def kv_sends(g):
        return [
            (me + 2 < n_ctx, kv_copy(g, 0, 2, 0, me + 2)),
            (me + 4 < n_ctx, kv_copy(g, 0, 4, 1, me + 4)),
            (even, kv_copy(g, 0, 1, 2, partner)),
        ]

    def kv_forwards(g):
        return [
            (2, even & (me >= 2), kv_copy(g, 2, 3, 3, partner)),
            (2, odd & (me >= 2), kv_copy(g, 2, 1, 3, partner)),
            (4, odd & (me >= 4), kv_copy(g, 4, 3, 4, partner)),
        ]

    def kv_wait(g, d):
        @pl.when(me >= d)
        def _():
            kv_copy(g, 0, d, 0, partner).wait_recv()

    def forward(g):
        for d in (2, 4):
            kv_wait(g, d)
            for source, cond, copy in kv_forwards(g):
                if source == d:
                    pl.when(cond)(copy.start)

    def exchange_copies(g):
        return [
            (even & (me >= 2), remote(gsend.at[g, SPAN - 1], xrecv.at[g, 0], x_ss.at[g, 0], x_rs.at[g, 0], partner)),
            (even & (me >= 2), remote(gsend.at[g, SPAN - 2], xrecv.at[g, 1], x_ss.at[g, 1], x_rs.at[g, 1], partner)),
            (odd & (me >= 4), remote(gsend.at[g, SPAN - 4], xrecv.at[g, 0], x_ss.at[g, 0], x_rs.at[g, 0], partner)),
            (odd, remote(gsend.at[g, SPAN - 1], grecv.at[g, 0], g_ss.at[g, 0], g_rs.at[g, 0], partner)),
            (even & (me >= 4), remote(gsend.at[g, SPAN - 4], grecv.at[g, 2], g_ss.at[g, 0], g_rs.at[g, 2], me - 4)),
        ]

    def final_copies(g):
        return [
            (even & (me >= 4), remote(csend.at[g, 0], grecv.at[g, 2], g_ss.at[g, 1], g_rs.at[g, 2], me - 3)),
            (odd & (me >= 2), remote(csend.at[g, 0], grecv.at[g, 1], g_ss.at[g, 1], g_rs.at[g, 1], me - 2)),
            (odd & (me >= 2), remote(csend.at[g, 1], grecv.at[g, 1], g_ss.at[g, 2], g_rs.at[g, 1], me - 3)),
        ]

    def combine(g):
        def add(i, d):
            both = gsend[g, SPAN - d].astype(jnp.float32) + xrecv[g, i].astype(jnp.float32)
            csend[g, i] = both.astype(jnp.bfloat16)

        @pl.when(even & (me >= 4))
        def _():
            exchange_copies(g)[2][1].wait_recv()
            add(0, 3)
            final_copies(g)[0][1].start()

        @pl.when(odd & (me >= 2))
        def _():
            exchange_copies(g)[0][1].wait_recv()
            add(0, 2)
            final_copies(g)[1][1].start()
            exchange_copies(g)[1][1].wait_recv()
            add(1, 3)
            final_copies(g)[2][1].start()

    def dq_out(g):
        cols = pl.ds(pl.multiple_of(g * (group * DH), DH), group * DH)
        return pltpu.make_async_copy(dq_ref.at[:, cols], dq_hbm.at[:, cols], out_s.at[g])

    for c in small_in():
        c.wait()
    starts = as_column(st_ref[...].astype(jnp.float32))
    slot_col = lax.broadcasted_iota(jnp.int32, (slots, 1), 0)
    ends = as_column(st_ref[...].astype(jnp.float32), 1)
    ends = ends + jnp.where(slot_col == slots - 1, jnp.float32(seq_len), 0.0)
    counts_row = ct_ref[...].astype(jnp.float32)
    counts = as_column(counts_row)
    lane = lax.broadcasted_iota(jnp.int32, (1, width), 1)
    for i in range(PAIR - 1, 0, -1):
        lane = jnp.where(lane >= i * tok, lane - i * tok, lane)
    pos = (me * tok + lane).astype(jnp.float32)
    in_doc = (pos >= starts) & (pos < ends)
    picked = (in_doc & (pos >= ends - counts)).astype(jnp.float32)
    part = jnp.sum(picked[:, :tok] * lr_ref[...], axis=1, keepdims=True)
    psend[...] = jnp.broadcast_to(part, (slots, 128))
    docs = jnp.sum((counts_row > 0).astype(jnp.float32), axis=1, keepdims=True)
    dsend[...] = jnp.broadcast_to(docs, (8, 128))
    for c in kv_in():
        c.wait()

    pl.semaphore_wait(
        barrier, jnp.minimum(me, SPAN) + jnp.minimum(n_ctx - 1 - me, SPAN) + (n_dp - 1)
    )

    def can_send(e):
        return me + e < n_ctx if e > 0 else me + e >= 0

    offsets = [e for e in range(-SPAN, SPAN + 1) if e != 0]
    for e in offsets:
        @pl.when(can_send(e))
        def _():
            part_copy(e).start()
    for k in range(1, n_dp):
        docs_copy(k).start()
    def send_kv(g):
        for cond, copy in kv_sends(g):
            pl.when(cond)(copy.start)

    send_kv(0)

    doc_lo = jnp.sum(jnp.where(in_doc, starts, 0.0), axis=0, keepdims=True)
    row = lax.broadcasted_iota(jnp.int32, (tok, 1), 0)
    tri = row <= lane
    near = (me * tok + row).astype(jnp.float32)
    near = jnp.where(tri, near, near - SPAN * tok)
    bias[0:tok] = jnp.where(near >= doc_lo, 0.0, -1e30)
    rest = lax.broadcasted_iota(jnp.int32, ((SPAN - 1) * tok, 1), 0) + (me - SPAN + 1) * tok
    bias[tok:] = jnp.where(rest.astype(jnp.float32) >= doc_lo, 0.0, -1e30)

    for e in offsets:
        @pl.when(can_send(-e))
        def _():
            part_copy(e).wait_recv()
    for k in range(1, n_dp):
        docs_copy(k).wait_recv()
    doc_sum = psend[...]
    for e in offsets:
        doc_sum = doc_sum + precv[SPAN - e]
    doc_sum = doc_sum[:, 0:1]
    total = dsend[...]
    for k in range(1, n_dp):
        total = total + drecv[k - 1]
    floored = jnp.maximum(counts, 1.0)
    prob = 1.0 / (1.0 + jnp.exp(-(doc_sum / floored)))
    coef = LOSS_SCALE * 2.0 * prob / (floored * total[0:1, 0:1])
    weight = jnp.sum(picked[:, :tok] * coef, axis=0, keepdims=True)
    wcol_ref[...] = jnp.broadcast_to(as_column(weight), (tok, 128))
    send_kv(1)
    forward(0)
    for c in big_in():
        c.wait()

    def one_group(g, carry):
        for d in (1, 3):
            kv_wait(g, d)
        @pl.when(g < HK - 2)
        def _():
            send_kv(g + 2)

        kt_buf[...] = kv_all[g, :, 0:DH].T
        acc[...] = jnp.zeros_like(acc)

        def one_pair(j, carry):
            first = (g * group + j * PAIR) * DH
            cols = [pl.ds(pl.multiple_of(first + i * DH, DH), DH) for i in range(PAIR)]
            keys = kv_all[g, :, 0:DH]
            vals = kv_all[g, :, DH:2 * DH]
            q2 = jnp.concatenate([q_ref[:, c] for c in cols], axis=0)
            wcol = wcol_ref[...]
            tri = lax.broadcasted_iota(jnp.int32, (tok, 1), 0) <= lane
            og2 = jnp.concatenate(
                [(wcol * up_ref[:, c].astype(jnp.float32)).astype(jnp.bfloat16) for c in cols],
                axis=0,
            )
            def merged(full):
                near = jnp.where(tri, full[SPAN * tok:], full[:tok])
                return jnp.concatenate([near, full[tok:SPAN * tok]], axis=0)

            def spread(x):
                far = jnp.where(tri, 0.0, x[:tok]).astype(jnp.bfloat16)
                own = jnp.where(tri, x[:tok], 0.0).astype(jnp.bfloat16)
                return jnp.concatenate([far, x[tok:].astype(jnp.bfloat16), own], axis=0)

            s = merged(dot_nt(keys, q2)) * (scale * LOG2E) + bias[...]
            e = jnp.exp2(s - jnp.max(s, axis=0, keepdims=True))
            inv = 1.0 / jnp.sum(e, axis=0, keepdims=True)
            p = e * inv
            dp = merged(dot_nt(vals, og2))
            delta = jnp.sum(p * dp, axis=0, keepdims=True)
            p_low = spread(p)
            ds = spread(p * (dp - delta))
            acc[:, 0:DH] += jnp.dot(ds, q2, preferred_element_type=jnp.float32)
            acc[:, DH:2 * DH] += jnp.dot(p_low, og2, preferred_element_type=jnp.float32)

            dqt = jnp.dot(kt_buf[...], ds, preferred_element_type=jnp.float32) * scale
            dq = dqt.T.astype(jnp.bfloat16)
            for i, c in enumerate(cols):
                dq_ref[:, c] = dq[i * tok:(i + 1) * tok]
            @pl.when((j == 0) & (g > 0))
            def _():
                combine(g - 1)

            @pl.when((j == group // PAIR - 2) & (g < HK - 1))
            def _():
                forward(g + 1)

            return carry

        lax.fori_loop(0, group // PAIR, one_pair, 0)
        dq_out(g).start()
        for d in range(1, SPAN + 1):
            lo = (SPAN - d) * tok
            gsend[g, SPAN - d, :, 0:DH] = (acc[lo:lo + tok, 0:DH] * scale).astype(jnp.bfloat16)
            gsend[g, SPAN - d, :, DH:2 * DH] = acc[lo:lo + tok, DH:2 * DH].astype(jnp.bfloat16)
        for cond, copy in exchange_copies(g):
            pl.when(cond)(copy.start)
        gown[g, :, 0:DH] = acc[SPAN * tok:, 0:DH] * scale
        gown[g, :, DH:2 * DH] = acc[SPAN * tok:, DH:2 * DH]
        return carry

    lax.fori_loop(0, HK, one_group, 0)
    combine(HK - 1)

    for g in range(HK):
        arrivals = ((0, even), (1, me - parity + 2 < n_ctx), (2, me - parity + 4 < n_ctx))
        for slot, cond in arrivals:
            @pl.when(cond)
            def _():
                remote(
                    csend.at[g, 0], grecv.at[g, slot], g_ss.at[g, 0], g_rs.at[g, slot], partner
                ).wait_recv()
                gown[g] += grecv[g, slot].astype(jnp.float32)
        out = gown[g].astype(jnp.bfloat16)
        dkv_ref[:, g * DH:(g + 1) * DH] = out[:, 0:DH]
        dkv_ref[:, (HK + g) * DH:(HK + g + 1) * DH] = out[:, DH:2 * DH]

    dkv_out = pltpu.make_async_copy(dkv_ref, dkv_hbm, out_s.at[HK])
    dkv_out.start()
    for e in offsets:
        @pl.when(can_send(e))
        def _():
            part_copy(e).wait_send()
    for k in range(1, n_dp):
        docs_copy(k).wait_send()
    for g in range(HK):
        sent = kv_sends(g) + [f[1:] for f in kv_forwards(g)] + exchange_copies(g) + final_copies(g)
        for cond, copy in sent:
            pl.when(cond)(copy.wait_send)
        dq_out(g).wait()
    dkv_out.wait()


def local(n_ctx, n_dp, query, key_value, upstream, log_ratio, doc_starts, answer_counts):
    tok = query.shape[1]
    slots = doc_starts.shape[1]
    window = (SPAN + 1) * tok
    f32, bf16 = jnp.float32, jnp.bfloat16
    sem = pltpu.SemaphoreType.DMA
    hbm = pl.BlockSpec(memory_space=pltpu.HBM)
    flops = 10 * HQ * tok * window * DH
    d_query, d_kv = pl.pallas_call(
        partial(kernel, n_ctx, n_dp),
        out_shape=(
            jax.ShapeDtypeStruct(query.shape[1:], bf16),
            jax.ShapeDtypeStruct(key_value.shape[1:], bf16),
        ),
        in_specs=[hbm] * 6,
        out_specs=(hbm, hbm),
        scratch_shapes=[
            pltpu.VMEM(query.shape[1:], bf16),
            pltpu.VMEM(key_value.shape[1:], bf16),
            pltpu.VMEM(query.shape[1:], bf16),
            pltpu.VMEM(upstream.shape[1:], bf16),
            pltpu.VMEM(log_ratio.shape, f32),
            pltpu.VMEM(doc_starts.shape, jnp.int32),
            pltpu.VMEM(answer_counts.shape, jnp.int32),
            pltpu.VMEM((HK, window, 2 * DH), bf16),
            pltpu.VMEM((DH, window), bf16),
            pltpu.VMEM((window - tok, PAIR * tok), f32),
            pltpu.VMEM((tok, 128), f32),
            pltpu.VMEM((window, 2 * DH), f32),
            pltpu.VMEM((HK, tok, 2 * DH), f32),
            pltpu.VMEM((HK, SPAN, tok, 2 * DH), bf16),
            pltpu.VMEM((HK, 2, tok, 2 * DH), bf16),
            pltpu.VMEM((HK, 2, tok, 2 * DH), bf16),
            pltpu.VMEM((HK, 3, tok, 2 * DH), bf16),
            pltpu.VMEM((slots, 128), f32),
            pltpu.VMEM((2 * SPAN + 1, slots, 128), f32),
            pltpu.VMEM((8, 128), f32),
            pltpu.VMEM((max(n_dp - 1, 1), 8, 128), f32),
            sem((5 + 2 * HK,)), sem((HK + 1,)), sem((HK, 5)), sem((HK, SPAN)),
            sem((HK, 2)), sem((HK, 2)), sem((HK, 3)), sem((HK, 3)),
            sem((2 * SPAN + 1,)), sem((2 * SPAN + 1,)),
            sem((max(n_dp - 1, 1),)), sem((max(n_dp - 1, 1),)),
        ],
        compiler_params=pltpu.CompilerParams(
            collective_id=0, has_side_effects=True, vmem_limit_bytes=64 * 1024 * 1024
        ),
        cost_estimate=pl.CostEstimate(
            flops=flops, bytes_accessed=8 * 1024 * 1024, transcendentals=HQ * tok * window
        ),
    )(query[0], key_value[0], upstream[0], log_ratio, doc_starts, answer_counts)
    return (d_query[None], d_kv[None])


def solution(mesh):
    n_ctx, n_dp = mesh.shape["ctx"], mesh.shape["dp"]
    return jax.shard_map(
        partial(local, n_ctx, n_dp),
        mesh=mesh,
        in_specs=(
            P("dp", "ctx", None),
            P("dp", "ctx", None),
            P("dp", "ctx", None),
            P("dp", "ctx"),
            P("dp", None),
            P("dp", None),
        ),
        out_specs=(P("dp", "ctx", None), P("dp", "ctx", None)),
        check_vma=False,
    )
```
